32 devices in a mesh: section: 4 (over y, core), seq: 8 (over z, x).
Axes of the slice: x: 2, y: 2, z: 4, core: 2. Of those that a mesh axis runs over, the one named last changes fastest.
Arguments:
- queries: bfloat16 [4, 1024, 2560], P('section', 'seq'), may hold values from -6 to 6
- cache_keys: bfloat16 [1024, 512], P('seq', 'section'), may hold values from -6 to 6
- cache_values: bfloat16 [1024, 512], P('seq', 'section'), may hold values from -6 to 6
- saved_out: bfloat16 [4, 1024, 2560], P('section', 'seq'), may hold values from -1.5 to 1.5
- out_grads: bfloat16 [4, 1024, 2560], P('section', 'seq'), may hold values from -6 to 6
- log_sums: bfloat16 [4, 1024, 20], P('section', 'seq')
Outputs:
- query_grads: bfloat16 [4, 1024, 2560], P('section', 'seq')
- key_grads: bfloat16 [1024, 512], P('seq', 'section')
- value_grads: bfloat16 [1024, 512], P('seq', 'section')
The draws below stay inside these ranges and needn't reach their ends.
All inputs are finite; a program needn't handle non-finite values.
Results may differ from the reference program's by a relative error of at most 0.0064.
Values may be sent and summed in bfloat16 or wider, within the bound.
No kernel may reach another device: no remote copies, remote signals or barrier semaphores. Data moves between devices by JAX's collectives and lax.ppermute only.
A program may use at most 64 MiB of HBM per device.

```python
import math
import jax
import jax.numpy as jnp
from jax import lax

HEADS = 20
KV_HEADS = 4
HEAD = 128
TOKENS = 1024
QPK = 5
LAYERS = 4


def draw_log_sums(key, part):
    key = jax.random.fold_in(key, 11)
    layout = (LAYERS, TOKENS, HEADS)
    position = lax.broadcasted_iota(jnp.float32, layout, 1)
    jitter = jax.random.uniform(key, layout, jnp.float32, 0.25, 0.75)
    return (jnp.log(position + 1.0) + jitter).astype(jnp.bfloat16)


def block_levels(rng, extent, cuts, least, high):
    factor_of = 1.0
    for axis_at, blocks in cuts:
        steps = jax.random.uniform(jax.random.fold_in(jax.random.fold_in(rng, 6), axis_at), (blocks,), jnp.float32, least / len(cuts), high / len(cuts))
        factor_of = factor_of * jnp.repeat(jnp.exp(steps), extent[axis_at] // blocks).reshape((-1,) + (1,) * (len(extent) - 1 - axis_at))
    return factor_of


def bell_draw(key, shape, deviation, most, split=(), kind=jnp.bfloat16):
    result = deviation * jax.random.normal(key, shape, jnp.float32)
    if split:
        result = result * block_levels(key, shape, split, -0.22, 0.18)
    return jnp.clip(result, -most, most).astype(kind)


def setup_inputs(seed: int = 0) -> dict:
    seeds = jax.random.split(jax.random.key(seed), 7)
    return {
        "queries": bell_draw(seeds[0], (LAYERS, TOKENS, HEADS * HEAD), 1.0, 6.0, ((0, 4), (1, 8))),
        "cache_keys": bell_draw(seeds[1], (TOKENS, KV_HEADS * HEAD), 1.0, 6.0, ((0, 8), (1, 4))),
        "cache_values": bell_draw(seeds[2], (TOKENS, KV_HEADS * HEAD), 1.0, 6.0, ((0, 8), (1, 4))),
        "saved_out": bell_draw(seeds[3], (LAYERS, TOKENS, HEADS * HEAD), 0.25, 1.5, ((0, 4), (1, 8))),
        "out_grads": bell_draw(seeds[4], (LAYERS, TOKENS, HEADS * HEAD), 1.0, 6.0, ((0, 4), (1, 8))),
        "log_sums": draw_log_sums(jax.random.fold_in(seeds[6], 71), 0),
    }


ROW_DIMS = (((1,), (1,)), ((), ()))
COL_DIMS = (((0,), (0,)), ((), ()))

def tile_terms(query_vecs, grad_vecs, total_vecs, row_dots, positions, key_tile, value_tile, key_start, inv_root):
    scores = lax.dot_general(query_vecs, key_tile, ROW_DIMS, preferred_element_type=jnp.float32) * inv_root
    key_pos = key_start + lax.broadcasted_iota(jnp.int32, (1, key_tile.shape[0]), 1)
    allowed = key_pos <= positions[:, None]
    weights = jnp.where(allowed, jnp.exp(scores - total_vecs[:, None]), 0.0)
    weights_low = weights.astype(jnp.bfloat16)
    weight_grads = lax.dot_general(grad_vecs, value_tile, ROW_DIMS, preferred_element_type=jnp.float32)
    score_grads = (weights * (weight_grads - row_dots[:, None]) * inv_root).astype(jnp.bfloat16)
    query_part = jnp.dot(score_grads, key_tile, preferred_element_type=jnp.float32)
    key_part = lax.dot_general(score_grads, query_vecs, COL_DIMS, preferred_element_type=jnp.float32)
    value_part = lax.dot_general(weights_low, grad_vecs, COL_DIMS, preferred_element_type=jnp.float32)
    return (query_part, key_part, value_part)

def add_rows(buffer, part, key_start):
    current = lax.dynamic_slice_in_dim(buffer, key_start, part.shape[0], 0)
    return lax.dynamic_update_slice_in_dim(buffer, current + part, key_start, 0)

def reference(queries, cache_keys, cache_values, saved_out, out_grads, log_sums):
    token_count = cache_keys.shape[0]
    tile_rows = min(512, token_count)
    tile_count = token_count // tile_rows
    inv_root = 1.0 / math.sqrt(HEAD)
    group_width = QPK * HEAD
    query_groups = []
    key_groups = []
    value_groups = []

    def regroup(array, width, offset):
        taken = array[:, :, offset:offset + width]
        return jnp.transpose(taken, (1, 0, 2)).reshape(tile_count, tile_rows, LAYERS, width)
    for group_index in range(KV_HEADS):
        query_tiles = regroup(queries, group_width, group_index * group_width)
        grad_tiles = regroup(out_grads, group_width, group_index * group_width)
        saved_tiles = regroup(saved_out, group_width, group_index * group_width)
        total_tiles = regroup(log_sums, QPK, group_index * QPK)
        key_group = cache_keys[:, group_index * HEAD:(group_index + 1) * HEAD]
        value_group = cache_values[:, group_index * HEAD:(group_index + 1) * HEAD]

        def visit(carry, inputs):
            key_sum, value_sum = carry
            tile_index, query_rows, grad_rows, saved_rows, total_rows = inputs
            query_vecs = query_rows.reshape(-1, HEAD)
            grad_vecs = grad_rows.reshape(-1, HEAD)
            products = grad_rows.astype(jnp.float32) * saved_rows.astype(jnp.float32)
            row_dots = lax.optimization_barrier(jnp.sum(products.reshape(-1, HEAD), axis=1))
            total_vecs = total_rows.reshape(-1).astype(jnp.float32)
            per_row = LAYERS * QPK
            positions = tile_index * tile_rows + lax.broadcasted_iota(jnp.int32, (query_vecs.shape[0],), 0) // per_row

            def sweep(key_index, state):
                query_acc, key_acc, value_acc = state
                key_start = (key_index * tile_rows).astype(jnp.int32)
                key_tile = lax.dynamic_slice_in_dim(key_group, key_start, tile_rows, 0)
                value_tile = lax.dynamic_slice_in_dim(value_group, key_start, tile_rows, 0)
                query_part, key_part, value_part = tile_terms(query_vecs, grad_vecs, total_vecs, row_dots, positions, key_tile, value_tile, key_start, inv_root)
                return (query_acc + query_part, add_rows(key_acc, key_part, key_start), add_rows(value_acc, value_part, key_start))
            query_acc = jnp.zeros((query_vecs.shape[0], HEAD), jnp.float32)
            query_acc, key_sum, value_sum = lax.fori_loop(0, tile_index + 1, sweep, (query_acc, key_sum, value_sum))
            return ((key_sum, value_sum), query_acc.reshape(tile_rows, LAYERS, group_width))
        initial = (jnp.zeros((token_count, HEAD), jnp.float32), jnp.zeros((token_count, HEAD), jnp.float32))
        indices = jnp.arange(tile_count, dtype=jnp.int32)
        (key_sum, value_sum), query_out = lax.scan(visit, initial, (indices, query_tiles, grad_tiles, saved_tiles, total_tiles))
        query_groups.append(jnp.transpose(query_out.reshape(token_count, LAYERS, group_width), (1, 0, 2)))
        key_groups.append(key_sum)
        value_groups.append(value_sum)
    query_grads = jnp.concatenate(query_groups, axis=2).astype(jnp.bfloat16)
    key_grads = jnp.concatenate(key_groups, axis=1).astype(jnp.bfloat16)
    value_grads = jnp.concatenate(value_groups, axis=1).astype(jnp.bfloat16)
    return (query_grads, key_grads, value_grads)
```

```python
import functools
import math

import jax
import jax.numpy as jnp
from jax import lax
from jax.experimental import pallas as pl
from jax.experimental.pallas import tpu as pltpu
from jax.sharding import PartitionSpec as P

NT_DIMS = (((1,), (1,)), ((), ()))
EXTRA = 4
VMEM_LIMIT = 32 * 1024 * 1024
SMEM = pl.BlockSpec(memory_space=pltpu.SMEM)
VMEM = pl.BlockSpec(memory_space=pltpu.VMEM)


def up16(rows):
    return -(-rows // 16) * 16


def pack_kernel(heads, head, places, queries, grads, saved, totals, *messages):
    rows = queries.shape[0]
    width = heads * head
    all_heads = queries.shape[1] // head
    lanes = lax.broadcasted_iota(jnp.int32, (rows, 128), 1)
    dots = jnp.zeros((rows, 128), jnp.float32)
    for h in range(all_heads):
        cols = slice(h * head, (h + 1) * head)
        product = grads[:, cols].astype(jnp.float32) * saved[:, cols].astype(jnp.float32)
        dots = jnp.where(lanes == h, jnp.sum(product, axis=1, keepdims=True), dots)
    dots_rows = jnp.transpose(dots)
    high = dots_rows.astype(jnp.bfloat16).astype(jnp.float32)
    rest = dots_rows - high
    middle = rest.astype(jnp.bfloat16).astype(jnp.float32)
    low = rest - middle
    padded = jnp.concatenate(
        [totals[...].astype(jnp.float32), jnp.zeros((rows, 128 - all_heads), jnp.float32)], axis=1
    )
    totals_rows = jnp.transpose(padded)
    parts = (totals_rows, high, middle, low)
    groups = all_heads // heads
    for k, message in enumerate(messages):
        place = places[k]
        start = pl.multiple_of(place * width, 128)
        for h in range(heads):
            at = pl.multiple_of(start + h * head, 128)
            message[h * rows : (h + 1) * rows, :] = queries[:, pl.ds(at, head)]
            message[(heads + h) * rows : (heads + h + 1) * rows, :] = grads[:, pl.ds(at, head)]
        blocks = []
        for part in parts:
            chosen = part[0:heads, :]
            for group in range(1, groups):
                chosen = jnp.where(
                    place == group, part[group * heads : (group + 1) * heads, :], chosen
                )
            blocks.append(chosen)
        extra = jnp.concatenate(blocks, axis=0)
        lines = message.shape[0] - 2 * heads * rows
        extra = jnp.concatenate(
            [extra, jnp.zeros((lines - extra.shape[0], 128), jnp.float32)], axis=0
        )
        message[2 * heads * rows :, :] = extra.astype(jnp.bfloat16)


def attend_kernel(layers, heads, head, outer, inv_root, info, *refs):
    messages = refs[:layers]
    own_blocks = refs[layers : layers + outer]
    other_blocks = refs[layers + outer]
    refs = refs[layers + outer + 1 :]
    query_outs = refs[:layers]
    mine, theirs = refs[layers : layers + 2]
    keys, values, query_all, grad_all, query_acc, sums = refs[layers + 2 :]
    rows = own_blocks[0].shape[0]
    pair = 2 * rows
    z, x = info[0], info[1]
    per_layer = heads * rows
    for k in range(outer):
        at = pl.multiple_of((z ^ k) * pair, pair)
        keys[pl.ds(at + x * rows, rows), :] = own_blocks[k][:, :head]
        values[pl.ds(at + x * rows, rows), :] = own_blocks[k][:, head:]
        keys[pl.ds(at + (1 - x) * rows, rows), :] = other_blocks[k, :, :head]
        values[pl.ds(at + (1 - x) * rows, rows), :] = other_blocks[k, :, head:]
    for layer in range(layers):
        there = slice(layer * per_layer, (layer + 1) * per_layer)
        query_all[there, :] = messages[layer][:per_layer, :]
        grad_all[there, :] = messages[layer][per_layer : 2 * per_layer, :]
    query_acc[...] = jnp.zeros_like(query_acc)
    chunks = [
        [(c // heads, c % heads) for c in range(i, min(i + 2, layers * heads))]
        for i in range(0, layers * heads, 2)
    ]

    def line(layer, h, part):
        at = 2 * per_layer + part * heads + h
        return messages[layer][at : at + 1, :].astype(jnp.float32)

    def sweep(j, masked):
        at = pl.multiple_of(j * pair, pair)
        key_tile = keys[pl.ds(at, pair), :]
        value_tile = values[pl.ds(at, pair), :]
        key_turned = jnp.transpose(key_tile)
        key_sum = jnp.zeros((pair, head), jnp.float32)
        value_sum = jnp.zeros((pair, head), jnp.float32)
        for chunk in chunks:
            first = (chunk[0][0] * heads + chunk[0][1]) * rows
            wide = len(chunk) * rows
            query = query_all[first : first + wide, :]
            grad = grad_all[first : first + wide, :]
            total = jnp.concatenate([line(a, b, 0) for a, b in chunk], axis=1)
            dot = jnp.concatenate(
                [line(a, b, 1) + (line(a, b, 2) + line(a, b, 3)) for a, b in chunk], axis=1
            )
            scores = lax.dot_general(key_tile, query, NT_DIMS, preferred_element_type=jnp.float32)
            weights = jnp.exp(scores * inv_root - total)
            if masked:
                key_pos = lax.broadcasted_iota(jnp.int32, (pair, wide), 0)
                query_pos = lax.broadcasted_iota(jnp.int32, (pair, wide), 1) % rows + x * rows
                weights = jnp.where(key_pos <= query_pos, weights, 0.0)
            weight_grads = lax.dot_general(
                value_tile, grad, NT_DIMS, preferred_element_type=jnp.float32
            )
            score_grads = (weights * (weight_grads - dot) * inv_root).astype(jnp.bfloat16)
            value_sum += jnp.dot(
                weights.astype(jnp.bfloat16), grad, preferred_element_type=jnp.float32
            )
            key_sum += jnp.dot(score_grads, query, preferred_element_type=jnp.float32)
            query_acc[:, first : first + wide] += jnp.dot(
                key_turned, score_grads, preferred_element_type=jnp.float32
            )
        sums[:, :head] = key_sum
        sums[:, head:] = value_sum
        place = j ^ z
        mine[place] = sums[pl.ds(pl.multiple_of(x * rows, rows), rows), :].astype(jnp.bfloat16)
        theirs[place] = sums[pl.ds(pl.multiple_of((1 - x) * rows, rows), rows), :].astype(
            jnp.bfloat16
        )

    def blank(j, carry):
        mine[j ^ z] = jnp.zeros(mine.shape[1:], jnp.bfloat16)
        theirs[j ^ z] = jnp.zeros(theirs.shape[1:], jnp.bfloat16)
        return carry

    def full(j, carry):
        sweep(j, False)
        return carry

    lax.fori_loop(0, z, full, 0)
    sweep(z, True)
    lax.fori_loop(z + 1, outer, blank, 0)
    for layer in range(layers):
        for h in range(heads):
            at = (layer * heads + h) * rows
            query_outs[layer][h * rows : (h + 1) * rows, :] = jnp.transpose(
                query_acc[:, at : at + rows]
            ).astype(jnp.bfloat16)


def add_kernel(mine, theirs, *outs):
    for k, out in enumerate(outs):
        out[...] = (mine[k].astype(jnp.float32) + theirs[k].astype(jnp.float32)).astype(
            jnp.bfloat16
        )


def place_kernel(heads, head, places, *refs):
    messages, out = refs[:-1], refs[-1]
    rows = out.shape[0]
    for k, message in enumerate(messages):
        start = pl.multiple_of(places[k] * heads * head, 128)
        for h in range(heads):
            at = pl.multiple_of(start + h * head, 128)
            out[:, pl.ds(at, head)] = message[h * rows : (h + 1) * rows, :]


def total_kernel(*refs):
    blocks, key_out, value_out = refs[:-2], refs[-2], refs[-1]
    total = blocks[0][...].astype(jnp.float32)
    for block in blocks[1:]:
        total = total + block[...].astype(jnp.float32)
    head = key_out.shape[1]
    key_out[...] = total[:, :head].astype(jnp.bfloat16)
    value_out[...] = total[:, head:].astype(jnp.bfloat16)


def call(kernel, outs, in_specs, scratch=()):
    return pl.pallas_call(
        kernel,
        out_shape=[jax.ShapeDtypeStruct(shape, jnp.bfloat16) for shape in outs],
        in_specs=in_specs,
        out_specs=[VMEM] * len(outs),
        scratch_shapes=list(scratch),
        compiler_params=pltpu.CompilerParams(vmem_limit_bytes=VMEM_LIMIT),
    )


def swap(array, axis, bits):
    size = lax.axis_size(axis)
    return lax.ppermute(array, axis, [(i, i ^ bits) for i in range(size)])


def local(queries, cache_keys, cache_values, saved_out, out_grads, log_sums):
    sections = lax.axis_size("section")
    seq = lax.axis_size("seq")
    outer = seq // 2
    section_at = lax.axis_index("section").astype(jnp.int32)
    seq_at = lax.axis_index("seq").astype(jnp.int32)
    rows, head = cache_keys.shape
    heads = log_sums.shape[2] // sections
    inv_root = 1.0 / math.sqrt(head)
    places = section_at ^ jnp.arange(sections, dtype=jnp.int32)
    info = jnp.stack([seq_at // 2, seq_at % 2])

    own = jnp.concatenate([cache_keys, cache_values], axis=1)
    own_blocks = [own] + [swap(own, "seq", 2 * k) for k in range(1, outer)]
    other_blocks = swap(jnp.stack(own_blocks), "seq", 1)

    lines = 2 * heads * rows + up16(EXTRA * heads)
    sent = call(
        functools.partial(pack_kernel, heads, head),
        [(lines, 128)] * sections,
        [SMEM] + [VMEM] * 4,
    )(places, queries[0], out_grads[0], saved_out[0], log_sums[0])
    messages = [sent[0]] + [swap(sent[k], "section", k) for k in range(1, sections)]

    results = call(
        functools.partial(attend_kernel, sections, heads, head, outer, inv_root),
        [(heads * rows, head)] * sections + [(outer, rows, 2 * head)] * 2,
        [SMEM] + [VMEM] * (sections + outer + 1),
        [
            pltpu.VMEM((seq * rows, head), jnp.bfloat16),
            pltpu.VMEM((seq * rows, head), jnp.bfloat16),
            pltpu.VMEM((sections * heads * rows, head), jnp.bfloat16),
            pltpu.VMEM((sections * heads * rows, head), jnp.bfloat16),
            pltpu.VMEM((head, sections * heads * rows), jnp.float32),
            pltpu.VMEM((2 * rows, 2 * head), jnp.float32),
        ],
    )(info, *messages, *own_blocks, other_blocks)
    mine, theirs = results[sections:]

    arrived = swap(theirs, "seq", 1)
    summed = call(add_kernel, [(rows, 2 * head)] * outer, [VMEM] * 2)(mine, arrived)
    blocks = [summed[0]] + [swap(summed[k], "seq", 2 * k) for k in range(1, outer)]
    key_grads, value_grads = call(total_kernel, [(rows, head)] * 2, [VMEM] * outer)(*blocks)

    back = [results[0]] + [swap(results[k], "section", k) for k in range(1, sections)]
    (query_grads,) = call(
        functools.partial(place_kernel, heads, head),
        [queries.shape[1:]],
        [SMEM] + [VMEM] * sections,
    )(places, *back)
    return (query_grads[None], key_grads, value_grads)


def solution(mesh):
    placed = (
        P("section", "seq", None),
        P("seq", "section"),
        P("seq", "section"),
        P("section", "seq", None),
        P("section", "seq", None),
        P("section", "seq", None),
    )
    return jax.shard_map(
        local,
        mesh=mesh,
        in_specs=placed,
        out_specs=(P("section", "seq", None), P("seq", "section"), P("seq", "section")),
        check_vma=False,
    )
```

```python
import functools
import math

import jax
import jax.numpy as jnp
from jax import lax
from jax.experimental import pallas as pl
from jax.experimental.pallas import tpu as pltpu
from jax.sharding import PartitionSpec as P

NT_DIMS = (((1,), (1,)), ((), ()))
UNROLLED = 4
EXTRA = 4
VMEM_LIMIT = 32 * 1024 * 1024
PACK_LIMIT = 62 * 1024 * 1024
LOG2E = math.log2(math.e)
SMEM = pl.BlockSpec(memory_space=pltpu.SMEM)
VMEM = pl.BlockSpec(memory_space=pltpu.VMEM)
HBM = pl.BlockSpec(memory_space=pltpu.HBM)


def up16(rows):
    return -(-rows // 16) * 16


def pack_kernel(heads, head, place_ref, queries, grads, saved, cache_keys, cache_values, totals, *refs):
    *messages, block, query_here, grad_here, saved_here, sems = refs
    rows = queries.shape[0]
    width = heads * head
    groups = queries.shape[1] // width
    pairs = [(grads, grad_here), (saved, saved_here), (queries, query_here)]
    pairs += [
        (cache_keys, block.at[:, pl.ds(0, head)]),
        (cache_values, block.at[:, pl.ds(head, head)]),
    ]
    loads = [
        pltpu.make_async_copy(source, target, sems.at[i]) for i, (source, target) in enumerate(pairs)
    ]
    for load in loads:
        load.start()
    loads[0].wait()
    loads[1].wait()
    lanes = lax.broadcasted_iota(jnp.int32, (rows, 128), 1)
    dots = jnp.zeros((rows, 128), jnp.float32)
    for h in range(groups * heads):
        cols = slice(h * head, (h + 1) * head)
        product = grad_here[:, cols].astype(jnp.float32) * saved_here[:, cols].astype(jnp.float32)
        dots = jnp.where(lanes == h, jnp.sum(product, axis=1, keepdims=True), dots)
    dots = jnp.transpose(dots)
    high = dots.astype(jnp.bfloat16).astype(jnp.float32)
    rest = dots - high
    middle = rest.astype(jnp.bfloat16).astype(jnp.float32)
    low = rest - middle
    parts = (totals[...].astype(jnp.float32), high, middle, low)
    for load in loads[2:]:
        load.wait()
    for k, message in enumerate(messages):
        place = place_ref[0] ^ k
        start = pl.multiple_of(place * width, 128)
        for h in range(heads):
            at = pl.multiple_of(start + h * head, 128)
            message[h * rows : (h + 1) * rows, :] = query_here[:, pl.ds(at, head)]
            message[(heads + h) * rows : (heads + h + 1) * rows, :] = grad_here[:, pl.ds(at, head)]
        lines = message.shape[0] - 2 * heads * rows
        extra = []
        for part in parts:
            chosen = part[0:heads, :]
            for group in range(1, groups):
                chosen = jnp.where(
                    place == group, part[group * heads : (group + 1) * heads, :], chosen
                )
            extra.append(chosen)
        extra.append(jnp.zeros((lines - EXTRA * heads, 128), jnp.float32))
        message[2 * heads * rows :, :] = jnp.concatenate(extra, axis=0).astype(jnp.bfloat16)


def attend_kernel(layers, heads, head, outer, first, last, inv_root, info, *refs):
    messages = refs[:layers]
    own_blocks = refs[layers : layers + outer]
    other_blocks = refs[layers + outer]
    refs = refs[layers + outer + 1 :]
    if not first:
        earlier, refs = refs[0], refs[1:]
    query_outs, refs = refs[:layers], refs[layers:]
    if last:
        mine, theirs = refs[:2]
        refs = refs[2:]
    else:
        partial, refs = refs[0], refs[1:]
    keys, values, query_turned, grad_turned, totals, dots, weights_all, score_all, query_acc = refs
    rows = own_blocks[0].shape[0]
    pair = 2 * rows
    z, x = info[0], info[1]
    per_layer = heads * rows
    every = layers * per_layer
    for k in range(outer):

        @pl.when(k <= z)
        def _():
            at = pl.multiple_of((z - k) * pair, pair)
            keys[pl.ds(at + x * rows, rows), :] = own_blocks[k][:, :head]
            values[pl.ds(at + x * rows, rows), :] = own_blocks[k][:, head:]
            keys[pl.ds(at + (1 - x) * rows, rows), :] = other_blocks[k, :, :head]
            values[pl.ds(at + (1 - x) * rows, rows), :] = other_blocks[k, :, head:]

    for layer in range(layers):
        there = slice(layer * per_layer, (layer + 1) * per_layer)
        query_turned[:, there] = jnp.transpose(messages[layer][:per_layer, :])
        grad_turned[:, there] = jnp.transpose(messages[layer][per_layer : 2 * per_layer, :])
        extra = messages[layer][2 * per_layer :, :].astype(jnp.float32)
        high, middle, low = (extra[i * heads : (i + 1) * heads] for i in (1, 2, 3))
        spare = jnp.zeros((128 - 2 * heads, 128), jnp.float32)
        columns = jnp.transpose(
            jnp.concatenate([extra[:heads] * LOG2E, high + (middle + low), spare], axis=0)
        )
        for h in range(heads):
            at = layer * per_layer + h * rows
            totals[at : at + rows, :] = jnp.broadcast_to(columns[:, h : h + 1], (rows, 128))
            dots[at : at + rows, :] = jnp.broadcast_to(
                columns[:, heads + h : heads + h + 1], (rows, 128)
            )
    chunks = [
        (layer, h, min(2, heads - h)) for layer in range(layers) for h in range(0, heads, 2)
    ]

    def tiles(at, spot, masked):
        key_tile = keys[pl.ds(at, pair), :]
        value_tile = values[pl.ds(at, pair), :]
        for layer, h, count in chunks:
            tall = count * rows
            top = layer * per_layer + h * rows
            here = slice(top, top + tall)
            query = messages[layer][h * rows : h * rows + tall, :]
            grad = messages[layer][per_layer + h * rows : per_layer + h * rows + tall, :]
            total = jnp.concatenate([totals[here, :]] * (pair // 128), axis=1)
            dot = jnp.concatenate([dots[here, :]] * (pair // 128), axis=1)
            scores = lax.dot_general(query, key_tile, NT_DIMS, preferred_element_type=jnp.float32)
            weights = jnp.exp2(scores * (inv_root * LOG2E) - total)
            if masked:
                key_pos = lax.broadcasted_iota(jnp.int32, (1, pair), 1)
                query_pos = lax.broadcasted_iota(jnp.int32, (tall, 1), 0) % rows + x * rows
                weights = jnp.where(key_pos <= query_pos, weights, 0.0)
            weight_grads = lax.dot_general(
                grad, value_tile, NT_DIMS, preferred_element_type=jnp.float32
            )
            score_grads = weights * (weight_grads - dot) * inv_root
            weights_all[here, spot : spot + pair] = weights.astype(jnp.bfloat16)
            score_all[here, spot : spot + pair] = score_grads.astype(jnp.bfloat16)

    def leave(j, key_sum, value_sum):
        if not first:
            key_sum += earlier[j, :, :pair]
            value_sum += earlier[j, :, pair:]
        if not last:
            partial[j, :, :pair] = key_sum
            partial[j, :, pair:] = value_sum
            return
        both = (jnp.transpose(key_sum), jnp.transpose(value_sum))
        for half, out in ((0, mine), (1, theirs)):
            for part, total in enumerate(both):
                chosen = jnp.where(x == half, total[:rows], total[rows:]).astype(jnp.bfloat16)
                out[z - j, :, part * head : (part + 1) * head] = chosen

    def sweep(j, masked):
        at = pl.multiple_of(j * pair, pair)
        tiles(at, 0, masked)
        here = slice(0, pair)
        query_acc[...] += jnp.dot(
            score_all[:, here], keys[pl.ds(at, pair), :], preferred_element_type=jnp.float32
        )
        leave(
            j,
            jnp.dot(query_turned[...], score_all[:, here], preferred_element_type=jnp.float32),
            jnp.dot(grad_turned[...], weights_all[:, here], preferred_element_type=jnp.float32),
        )

    def full(j, carry):
        sweep(j, False)
        return carry

    def stepwise():
        query_acc[...] = jnp.zeros_like(query_acc)
        lax.fori_loop(0, z, full, 0)
        sweep(z, True)
        for layer in range(layers):
            query_outs[layer][...] = query_acc[
                layer * per_layer : (layer + 1) * per_layer, :
            ].astype(jnp.bfloat16)

    def whole():
        for j in range(outer):
            tiles(j * pair, j * pair, j == outer - 1)
        key_sum = jnp.dot(query_turned[...], score_all[...], preferred_element_type=jnp.float32)
        value_sum = jnp.dot(grad_turned[...], weights_all[...], preferred_element_type=jnp.float32)
        for j in range(outer):
            here = slice(j * pair, (j + 1) * pair)
            leave(j, key_sum[:, here], value_sum[:, here])
        for layer in range(layers):
            there = slice(layer * per_layer, (layer + 1) * per_layer)
            query_outs[layer][...] = jnp.dot(
                score_all[there, :], keys[...], preferred_element_type=jnp.float32
            ).astype(jnp.bfloat16)

    if outer <= UNROLLED:
        pl.when(z == outer - 1)(whole)
        pl.when(z < outer - 1)(stepwise)
    else:
        stepwise()
    if last:

        def blank(k, carry):
            mine[k] = jnp.zeros(mine.shape[1:], jnp.bfloat16)
            theirs[k] = jnp.zeros(theirs.shape[1:], jnp.bfloat16)
            return carry

        lax.fori_loop(z + 1, outer, blank, 0)


def add_kernel(mine, theirs, *outs):
    for k, out in enumerate(outs):
        out[...] = (mine[k].astype(jnp.float32) + theirs[k].astype(jnp.float32)).astype(
            jnp.bfloat16
        )


def place_kernel(heads, head, place_ref, *refs):
    messages, out = refs[:-1], refs[-1]
    rows = out.shape[0]
    for k, message in enumerate(messages):
        start = pl.multiple_of((place_ref[0] ^ k) * heads * head, 128)
        for h in range(heads):
            at = pl.multiple_of(start + h * head, 128)
            out[:, pl.ds(at, head)] = message[h * rows : (h + 1) * rows, :]


def total_kernel(*refs):
    blocks, key_out, value_out = refs[:-2], refs[-2], refs[-1]
    total = blocks[0][...].astype(jnp.float32)
    for block in blocks[1:]:
        total = total + block[...].astype(jnp.float32)
    head = key_out.shape[1]
    key_out[...] = total[:, :head].astype(jnp.bfloat16)
    value_out[...] = total[:, head:].astype(jnp.bfloat16)


def call(kernel, outs, in_specs, scratch=(), kinds=None, limit=VMEM_LIMIT):
    kinds = kinds or [jnp.bfloat16] * len(outs)
    return pl.pallas_call(
        kernel,
        out_shape=[jax.ShapeDtypeStruct(shape, kind) for shape, kind in zip(outs, kinds)],
        in_specs=in_specs,
        out_specs=[VMEM] * len(outs),
        scratch_shapes=list(scratch),
        compiler_params=pltpu.CompilerParams(vmem_limit_bytes=limit),
    )


def swap(array, axis, bits):
    size = lax.axis_size(axis)
    return lax.ppermute(array, axis, [(i, i ^ bits) for i in range(size)])


def move(array, step):
    size = lax.axis_size("seq")
    return lax.ppermute(
        array, "seq", [(i, i + step) for i in range(size) if 0 <= i + step < size]
    )


def local(queries, cache_keys, cache_values, saved_out, out_grads, log_sums):
    sections = lax.axis_size("section")
    seq = lax.axis_size("seq")
    outer = seq // 2
    section_at = lax.axis_index("section").astype(jnp.int32).reshape(1)
    seq_at = lax.axis_index("seq").astype(jnp.int32)
    rows, head = cache_keys.shape
    heads = log_sums.shape[2] // sections
    inv_root = 1.0 / math.sqrt(head)
    info = jnp.stack([seq_at // 2, seq_at % 2])
    lines = 2 * heads * rows + up16(EXTRA * heads)

    *sent, own = call(
        functools.partial(pack_kernel, heads, head),
        [(lines, 128)] * sections + [(rows, 2 * head)],
        [SMEM] + [HBM] * 5 + [VMEM],
        [pltpu.VMEM(queries.shape[1:], jnp.bfloat16)] * 3 + [pltpu.SemaphoreType.DMA((5,))],
        limit=PACK_LIMIT,
    )(
        section_at,
        queries[0],
        out_grads[0],
        saved_out[0],
        cache_keys,
        cache_values,
        jnp.transpose(log_sums[0]),
    )
    messages = [sent[0]] + [swap(sent[k], "section", k) for k in range(1, sections)]
    own_blocks = [own] + [move(own, 2 * k) for k in range(1, outer)]
    other_blocks = swap(jnp.stack(own_blocks), "seq", 1)

    def attend(which, first, last, earlier=()):
        count = len(which)
        outs = [(heads * rows, head)] * count
        kinds = [jnp.bfloat16] * count
        if last:
            outs, kinds = outs + [(outer, rows, 2 * head)] * 2, kinds + [jnp.bfloat16] * 2
        else:
            outs, kinds = outs + [(outer, head, 4 * rows)], kinds + [jnp.float32]
        every = count * heads * rows
        across = 2 * rows * (outer if outer <= UNROLLED else 1)
        return call(
            functools.partial(attend_kernel, count, heads, head, outer, first, last, inv_root),
            outs,
            [SMEM] + [VMEM] * (count + outer + 1 + len(earlier)),
            [pltpu.VMEM((seq * rows, head), jnp.bfloat16)] * 2
            + [pltpu.VMEM((head, every), jnp.bfloat16)] * 2
            + [pltpu.VMEM((every, 128), jnp.float32)] * 2
            + [pltpu.VMEM((every, across), jnp.bfloat16)] * 2
            + [pltpu.VMEM((every, head), jnp.float32)],
            kinds,
        )(info, *[messages[k] for k in which], *own_blocks, other_blocks, *earlier)

    late = sections - 1
    early = tuple(k for k in range(sections) if k != late)
    *grads, partial = attend(early, True, False)
    back = dict(zip(early, grads))
    back[late], mine, theirs = attend((late,), False, True, (partial,))

    arrived = swap(theirs, "seq", 1)
    summed = call(add_kernel, [(rows, 2 * head)] * outer, [VMEM] * 2)(mine, arrived)
    blocks = [summed[0]] + [move(summed[k], -2 * k) for k in range(1, outer)]
    key_grads, value_grads = call(total_kernel, [(rows, head)] * 2, [VMEM] * outer)(*blocks)

    back = [back[0]] + [swap(back[k], "section", k) for k in range(1, sections)]
    (query_grads,) = call(
        functools.partial(place_kernel, heads, head),
        [queries.shape[1:]],
        [SMEM] + [VMEM] * sections,
    )(section_at, *back)
    return (query_grads[None], key_grads, value_grads)


def solution(mesh):
    placed = (
        P("section", "seq", None),
        P("seq", "section"),
        P("seq", "section"),
        P("section", "seq", None),
        P("section", "seq", None),
        P("section", "seq", None),
    )
    return jax.shard_map(
        local,
        mesh=mesh,
        in_specs=placed,
        out_specs=(P("section", "seq", None), P("seq", "section"), P("seq", "section")),
        check_vma=False,
    )
```

```python
import functools
import math

import jax
import jax.numpy as jnp
from jax import lax
from jax.experimental import pallas as pl
from jax.experimental.pallas import tpu as pltpu
from jax.sharding import PartitionSpec as P

NT_DIMS = (((1,), (1,)), ((), ()))
UNROLLED = 4
EXTRA = 4
VMEM_LIMIT = 32 * 1024 * 1024
PACK_LIMIT = 62 * 1024 * 1024
LOG2E = math.log2(math.e)
SMEM = pl.BlockSpec(memory_space=pltpu.SMEM)
VMEM = pl.BlockSpec(memory_space=pltpu.VMEM)
HBM = pl.BlockSpec(memory_space=pltpu.HBM)


def up16(rows):
    return -(-rows // 16) * 16


def pack_kernel(heads, head, which, cached, after, place_ref, queries, grads, saved, totals, *refs):
    cache, refs = refs[:cached], refs[cached + after :]
    outs, refs = refs[: len(which)], refs[len(which) :]
    block, refs = (refs[0], refs[1:]) if cached else (None, refs)
    here, totals_here, ready, sems = refs
    rows = queries.shape[0]
    width = heads * head
    groups = queries.shape[1] // width
    ends = []
    for m, k in enumerate(which):
        columns = pl.ds(pl.multiple_of((place_ref[0] ^ k) * width, 128), width)
        for i, source in enumerate((grads, saved, queries)):
            ends.append((source.at[:, columns], here.at[m, i]))
    ends.append((totals, totals_here))
    for i, source in enumerate(cache):
        ends.append((source, block.at[:, pl.ds(i * head, head)]))
    loads = [pltpu.make_async_copy(*pair, sems.at[i]) for i, pair in enumerate(ends)]
    stores = [
        pltpu.make_async_copy(ready.at[m], out, sems.at[len(loads) + m])
        for m, out in enumerate(outs)
    ]
    for load in loads:
        load.start()
    lanes = lax.broadcasted_iota(jnp.int32, (rows, 128), 1)
    for m, k in enumerate(which):
        message = ready.at[m]
        for load in loads[3 * m : 3 * m + 3]:
            load.wait()
        dots = jnp.zeros((rows, 128), jnp.float32)
        for h in range(heads):
            columns = slice(h * head, (h + 1) * head)
            grad = here[m, 0, :, columns]
            out = here[m, 1, :, columns].astype(jnp.float32)
            product = grad.astype(jnp.float32) * out
            dots = jnp.where(lanes == h, jnp.sum(product, axis=1, keepdims=True), dots)
            message[h * rows : (h + 1) * rows, :] = here[m, 2, :, columns]
            message[(heads + h) * rows : (heads + h + 1) * rows, :] = grad
        dots = jnp.transpose(dots)[:heads]
        high = dots.astype(jnp.bfloat16).astype(jnp.float32)
        rest = dots - high
        middle = rest.astype(jnp.bfloat16).astype(jnp.float32)
        low = rest - middle
        if m == 0:
            loads[3 * len(which)].wait()
        chosen = totals_here[0:heads, :].astype(jnp.float32)
        for group in range(1, groups):
            part = totals_here[group * heads : (group + 1) * heads, :].astype(jnp.float32)
            chosen = jnp.where((place_ref[0] ^ k) == group, part, chosen)
        spare = jnp.zeros((message.shape[0] - 2 * heads * rows - EXTRA * heads, 128), jnp.float32)
        extra = jnp.concatenate([chosen, high, middle, low, spare], axis=0)
        message[2 * heads * rows :, :] = extra.astype(jnp.bfloat16)
        stores[m].start()
    for copy in loads[3 * len(which) + 1 :] + stores:
        copy.wait()


def attend_kernel(layers, heads, head, outer, inv_root, info, *refs):
    messages = refs[:layers]
    own, own_swapped, further, others = refs[layers : layers + 4]
    refs = refs[layers + 4 :]
    halves, refs = refs[:4], refs[4:]
    query_outs, refs = refs[:layers], refs[layers:]
    keys, values, query_turned, grad_turned, totals, dots, weights_all, score_all, query_acc = refs
    rows = own.shape[0]
    pair = 2 * rows
    z, x = info[0], info[1]
    near = outer // 2
    per_layer = heads * rows
    every = layers * per_layer
    for k in range(outer):
        at = pl.multiple_of((z ^ k) * pair, pair)
        here, there = (further.at[k - 1], others.at[k - 1]) if k else (own, own_swapped)
        for block, half in ((here, x), (there, 1 - x)):
            keys[pl.ds(at + half * rows, rows), :] = block[:, :head]
            values[pl.ds(at + half * rows, rows), :] = block[:, head:]

    for layer in range(layers):
        there = slice(layer * per_layer, (layer + 1) * per_layer)
        query_turned[:, there] = jnp.transpose(messages[layer][:per_layer, :])
        grad_turned[:, there] = jnp.transpose(messages[layer][per_layer : 2 * per_layer, :])
        extra = messages[layer][2 * per_layer :, :].astype(jnp.float32)
        high, middle, low = (extra[i * heads : (i + 1) * heads] for i in (1, 2, 3))
        spare = jnp.zeros((128 - 2 * heads, 128), jnp.float32)
        columns = jnp.transpose(
            jnp.concatenate([extra[:heads] * LOG2E, high + (middle + low), spare], axis=0)
        )
        for h in range(heads):
            at = layer * per_layer + h * rows
            totals[at : at + rows, :] = jnp.broadcast_to(columns[:, h : h + 1], (rows, 128))
            dots[at : at + rows, :] = jnp.broadcast_to(
                columns[:, heads + h : heads + h + 1], (rows, 128)
            )
    chunks = [
        (layer, h, min(2, heads - h)) for layer in range(layers) for h in range(0, heads, 2)
    ]

    def tiles(at, columns, masked):
        key_tile = keys[pl.ds(at, pair), :]
        value_tile = values[pl.ds(at, pair), :]
        for layer, h, count in chunks:
            tall = count * rows
            top = layer * per_layer + h * rows
            here = slice(top, top + tall)
            query = messages[layer][h * rows : h * rows + tall, :]
            grad = messages[layer][per_layer + h * rows : per_layer + h * rows + tall, :]
            total = jnp.concatenate([totals[here, :]] * (pair // 128), axis=1)
            dot = jnp.concatenate([dots[here, :]] * (pair // 128), axis=1)
            scores = lax.dot_general(query, key_tile, NT_DIMS, preferred_element_type=jnp.float32)
            weights = jnp.exp2(scores * (inv_root * LOG2E) - total)
            if masked:
                key_pos = lax.broadcasted_iota(jnp.int32, (1, pair), 1)
                query_pos = lax.broadcasted_iota(jnp.int32, (tall, 1), 0) % rows + x * rows
                weights = jnp.where(key_pos <= query_pos, weights, 0.0)
            weight_grads = lax.dot_general(
                grad, value_tile, NT_DIMS, preferred_element_type=jnp.float32
            )
            score_grads = weights * (weight_grads - dot) * inv_root
            weights_all[here, columns] = weights.astype(jnp.bfloat16)
            score_all[here, columns] = score_grads.astype(jnp.bfloat16)

    def leave(j, key_sum, value_sum):
        both = (jnp.transpose(key_sum), jnp.transpose(value_sum))
        step = z - j
        for half in range(2):
            chosen = jnp.concatenate(
                [jnp.where(x == half, total[:rows], total[rows:]) for total in both], axis=1
            ).astype(jnp.bfloat16)

            @pl.when(step < near)
            def _():
                halves[2 * half][step] = chosen

            @pl.when(step >= near)
            def _():
                halves[2 * half + 1][step - near] = chosen

    def sweep(j, masked):
        at = pl.multiple_of(j * pair, pair)
        here = slice(0, pair)
        tiles(at, here, masked)
        query_acc[...] += jnp.dot(
            score_all[:, here], keys[pl.ds(at, pair), :], preferred_element_type=jnp.float32
        )
        leave(
            j,
            jnp.dot(query_turned[...], score_all[:, here], preferred_element_type=jnp.float32),
            jnp.dot(grad_turned[...], weights_all[:, here], preferred_element_type=jnp.float32),
        )

    def full(j, carry):
        sweep(j, False)
        return carry

    def stepwise():
        query_acc[...] = jnp.zeros_like(query_acc)
        lax.fori_loop(0, z, full, 0)
        sweep(z, True)
        for layer in range(layers):
            query_outs[layer][...] = query_acc[
                layer * per_layer : (layer + 1) * per_layer, :
            ].astype(jnp.bfloat16)

    def whole():
        for j in range(outer):
            here = slice(j * pair, (j + 1) * pair)
            tiles(j * pair, here, j == outer - 1)
        key_sum = jnp.dot(query_turned[...], score_all[...], preferred_element_type=jnp.float32)
        value_sum = jnp.dot(grad_turned[...], weights_all[...], preferred_element_type=jnp.float32)
        for j in range(outer):
            here = slice(j * pair, (j + 1) * pair)
            leave(j, key_sum[:, here], value_sum[:, here])
        for layer in range(layers):
            there = slice(layer * per_layer, (layer + 1) * per_layer)
            query_outs[layer][...] = jnp.dot(
                score_all[there, :], keys[...], preferred_element_type=jnp.float32
            ).astype(jnp.bfloat16)

    if outer <= UNROLLED:
        pl.when(z == outer - 1)(whole)
        pl.when(z < outer - 1)(stepwise)
    else:
        stepwise()

    def blank(out, first):
        def body(k, carry):
            out[k - first] = jnp.zeros(out.shape[1:], jnp.bfloat16)
            return carry

        lax.fori_loop(jnp.maximum(z + 1, first), first + out.shape[0], body, 0)

    for half in range(2):
        blank(halves[2 * half], 0)
        blank(halves[2 * half + 1], near)


def add_kernel(mine, theirs, *outs):
    for k, out in enumerate(outs):
        out[...] = (mine[k].astype(jnp.float32) + theirs[k].astype(jnp.float32)).astype(
            jnp.bfloat16
        )


def place_kernel(heads, head, place_ref, *refs):
    messages, out = refs[:-1], refs[-1]
    rows = out.shape[0]
    for k, message in enumerate(messages):
        start = pl.multiple_of((place_ref[0] ^ k) * heads * head, 128)
        for h in range(heads):
            at = pl.multiple_of(start + h * head, 128)
            out[:, pl.ds(at, head)] = message[h * rows : (h + 1) * rows, :]


def total_kernel(*refs):
    blocks, key_out, value_out = refs[:-2], refs[-2], refs[-1]
    total = blocks[0][...].astype(jnp.float32)
    for block in blocks[1:]:
        total = total + block[...].astype(jnp.float32)
    head = key_out.shape[1]
    key_out[...] = total[:, :head].astype(jnp.bfloat16)
    value_out[...] = total[:, head:].astype(jnp.bfloat16)


def call(kernel, outs, in_specs, scratch=(), limit=VMEM_LIMIT, out_specs=None):
    return pl.pallas_call(
        kernel,
        out_shape=[jax.ShapeDtypeStruct(shape, jnp.bfloat16) for shape in outs],
        in_specs=in_specs,
        out_specs=out_specs or [VMEM] * len(outs),
        scratch_shapes=list(scratch),
        compiler_params=pltpu.CompilerParams(vmem_limit_bytes=limit),
    )


def swap(array, axis, bits):
    size = lax.axis_size(axis)
    return lax.ppermute(array, axis, [(i, i ^ bits) for i in range(size)])


def move(array, step):
    size = lax.axis_size("seq")
    return lax.ppermute(
        array, "seq", [(i, i + step) for i in range(size) if 0 <= i + step < size]
    )


def local(queries, cache_keys, cache_values, saved_out, out_grads, log_sums):
    sections = lax.axis_size("section")
    seq = lax.axis_size("seq")
    outer = seq // 2
    section_at = lax.axis_index("section").astype(jnp.int32).reshape(1)
    seq_at = lax.axis_index("seq").astype(jnp.int32)
    rows, head = cache_keys.shape
    heads = log_sums.shape[2] // sections
    inv_root = 1.0 / math.sqrt(head)
    info = jnp.stack([seq_at // 2, seq_at % 2])
    lines = 2 * heads * rows + up16(EXTRA * heads)

    totals = jnp.transpose(log_sums[0])

    half = sections // 2
    *sent, own = call(
        functools.partial(pack_kernel, heads, head, tuple(range(sections)), 2, 0),
        [(lines, 128)] * sections + [(rows, 2 * head)],
        [SMEM] + [HBM] * 6,
        [
            pltpu.VMEM((sections, 3, rows, heads * head), jnp.bfloat16),
            pltpu.VMEM(totals.shape, jnp.bfloat16),
            pltpu.VMEM((sections, lines, 128), jnp.bfloat16),
            pltpu.SemaphoreType.DMA((4 * sections + 3,)),
        ],
        limit=PACK_LIMIT,
        out_specs=[HBM] * (sections + 1),
    )(section_at, queries[0], out_grads[0], saved_out[0], totals, cache_keys, cache_values)
    passed = swap(sent[half + 1], "section", 1)
    messages = [sent[0], swap(sent[1], "section", 1), swap(sent[half], "section", half)]
    passed, tied = lax.optimization_barrier((passed, own))
    messages.append(swap(passed, "section", half))

    def exchange(own):
        far = {k: swap(own, "seq", 2 * k) for k in reversed(range(1, outer))}
        return jnp.stack([far[k] for k in range(1, outer)])

    def nothing(own):
        return jnp.zeros((outer - 1, *own.shape), own.dtype)

    further = lax.cond(seq_at >= 0, exchange, nothing, tied)
    blocks_here = [own, swap(own, "seq", 1), further, swap(further, "seq", 1)]

    every = sections * heads * rows
    across = 2 * rows * (outer if outer <= UNROLLED else 1)
    bf16 = functools.partial(pltpu.VMEM, dtype=jnp.bfloat16)
    mine_near, mine_far, theirs_near, theirs_far, *back = call(
        functools.partial(attend_kernel, sections, heads, head, outer, inv_root),
        [(outer // 2, rows, 2 * head), (outer - outer // 2, rows, 2 * head)] * 2
        + [(heads * rows, head)] * sections,
        [SMEM] + [VMEM] * (sections + 4),
        [bf16((seq * rows, head))] * 2
        + [bf16((head, every))] * 2
        + [pltpu.VMEM((every, 128), jnp.float32)] * 2
        + [bf16((every, across))] * 2
        + [pltpu.VMEM((every, head), jnp.float32)],
    )(info, *messages, *blocks_here)

    def reduced(mine, theirs):
        count = mine.shape[0]
        return call(add_kernel, [(rows, 2 * head)] * count, [VMEM] * 2)(
            mine, swap(theirs, "seq", 1)
        )

    far_sums = reduced(mine_far, theirs_far)
    summed = [*reduced(mine_near, theirs_near), *far_sums]
    blocks = [move(summed[k], -2 * k) for k in reversed(range(1, outer))] + [summed[0]]
    key_grads, value_grads = call(total_kernel, [(rows, head)] * 2, [VMEM] * outer)(*blocks)

    back = [back[0]] + [swap(back[k], "section", k) for k in range(1, sections)]
    (query_grads,) = call(
        functools.partial(place_kernel, heads, head),
        [queries.shape[1:]],
        [SMEM] + [VMEM] * sections,
    )(section_at, *back)
    return (query_grads[None], key_grads, value_grads)


def solution(mesh):
    placed = (
        P("section", "seq", None),
        P("seq", "section"),
        P("seq", "section"),
        P("section", "seq", None),
        P("section", "seq", None),
        P("section", "seq", None),
    )
    return jax.shard_map(
        local,
        mesh=mesh,
        in_specs=placed,
        out_specs=(P("section", "seq", None), P("seq", "section"), P("seq", "section")),
        check_vma=False,
    )
```

```python
import functools
import math

import jax
import jax.numpy as jnp
from jax import lax
from jax.experimental import pallas as pl
from jax.experimental.pallas import tpu as pltpu
from jax.sharding import PartitionSpec as P

NT_DIMS = (((1,), (1,)), ((), ()))
UNROLLED = 4
EXTRA = 4
VMEM_LIMIT = 32 * 1024 * 1024
PACK_LIMIT = 62 * 1024 * 1024
LOG2E = math.log2(math.e)
SMEM = pl.BlockSpec(memory_space=pltpu.SMEM)
VMEM = pl.BlockSpec(memory_space=pltpu.VMEM)
HBM = pl.BlockSpec(memory_space=pltpu.HBM)


def up16(rows):
    return -(-rows // 16) * 16


def pack_kernel(heads, head, which, cached, after, place_ref, queries, grads, saved, totals, *refs):
    cache, refs = refs[:cached], refs[cached + after :]
    outs, refs = refs[: len(which)], refs[len(which) :]
    block, refs = (refs[0], refs[1:]) if cached else (None, refs)
    here, totals_here, ready, sems = refs
    rows = queries.shape[0]
    width = heads * head
    groups = queries.shape[1] // width
    ends = []
    for m, k in enumerate(which):
        columns = pl.ds(pl.multiple_of((place_ref[0] ^ k) * width, 128), width)
        for i, source in enumerate((grads, saved, queries)):
            ends.append((source.at[:, columns], here.at[m, i]))
    ends.append((totals, totals_here))
    for i, source in enumerate(cache):
        ends.append((source, block.at[:, pl.ds(i * head, head)]))
    loads = [pltpu.make_async_copy(*pair, sems.at[i]) for i, pair in enumerate(ends)]
    stores = [
        pltpu.make_async_copy(ready.at[m], out, sems.at[len(loads) + m])
        for m, out in enumerate(outs)
    ]
    for load in loads:
        load.start()
    lanes = lax.broadcasted_iota(jnp.int32, (rows, 128), 1)
    for m, k in enumerate(which):
        message = ready.at[m]
        for load in loads[3 * m : 3 * m + 3]:
            load.wait()
        dots = jnp.zeros((rows, 128), jnp.float32)
        for h in range(heads):
            columns = slice(h * head, (h + 1) * head)
            grad = here[m, 0, :, columns]
            out = here[m, 1, :, columns].astype(jnp.float32)
            product = grad.astype(jnp.float32) * out
            dots = jnp.where(lanes == h, jnp.sum(product, axis=1, keepdims=True), dots)
            message[h * rows : (h + 1) * rows, :] = here[m, 2, :, columns]
            message[(heads + h) * rows : (heads + h + 1) * rows, :] = grad
        dots = jnp.transpose(dots)[:heads]
        high = dots.astype(jnp.bfloat16).astype(jnp.float32)
        rest = dots - high
        middle = rest.astype(jnp.bfloat16).astype(jnp.float32)
        low = rest - middle
        if m == 0:
            loads[3 * len(which)].wait()
        chosen = totals_here[0:heads, :].astype(jnp.float32)
        for group in range(1, groups):
            part = totals_here[group * heads : (group + 1) * heads, :].astype(jnp.float32)
            chosen = jnp.where((place_ref[0] ^ k) == group, part, chosen)
        spare = jnp.zeros((message.shape[0] - 2 * heads * rows - EXTRA * heads, 128), jnp.float32)
        extra = jnp.concatenate([chosen, high, middle, low, spare], axis=0)
        message[2 * heads * rows :, :] = extra.astype(jnp.bfloat16)
        stores[m].start()
    for copy in loads[3 * len(which) + 1 :] + stores:
        copy.wait()


def attend_kernel(layers, heads, head, outer, inv_root, info, *refs):
    messages = refs[:layers]
    own, own_swapped, further, others = refs[layers : layers + 4]
    refs = refs[layers + 4 :]
    halves, refs = refs[:4], refs[4:]
    query_outs, refs = refs[:layers], refs[layers:]
    keys, values, query_turned, grad_turned, totals, dots, weights_all, score_all, *refs = refs
    rows = own.shape[0]
    pair = 2 * rows
    z, x = info[0], info[1]
    near = outer // 2
    per_layer = heads * rows
    every = layers * per_layer
    for k in range(outer):
        at = pl.multiple_of((z ^ k) * pair, pair)
        here, there = (further.at[k - 1], others.at[k - 1]) if k else (own, own_swapped)
        for block, half in ((here, x), (there, 1 - x)):
            keys[pl.ds(at + half * rows, rows), :] = block[:, :head]
            values[pl.ds(at + half * rows, rows), :] = block[:, head:]

    for layer in range(layers):
        there = slice(layer * per_layer, (layer + 1) * per_layer)
        query_turned[:, there] = jnp.transpose(messages[layer][:per_layer, :])
        grad_turned[:, there] = jnp.transpose(messages[layer][per_layer : 2 * per_layer, :])
        extra = messages[layer][2 * per_layer :, :].astype(jnp.float32)
        high, middle, low = (extra[i * heads : (i + 1) * heads] for i in (1, 2, 3))
        spare = jnp.zeros((128 - 2 * heads, 128), jnp.float32)
        columns = jnp.transpose(
            jnp.concatenate([extra[:heads] * LOG2E, high + (middle + low), spare], axis=0)
        )
        for h in range(heads):
            at = layer * per_layer + h * rows
            totals[at : at + rows, :] = jnp.broadcast_to(columns[:, h : h + 1], (rows, 128))
            dots[at : at + rows, :] = jnp.broadcast_to(
                columns[:, heads + h : heads + h + 1], (rows, 128)
            )
    chunks = [
        (layer, h, min(2, heads - h)) for layer in range(layers) for h in range(0, heads, 2)
    ]

    def tiles(at, columns, masked, turned=None):
        key_tile = keys[pl.ds(at, pair), :]
        value_tile = values[pl.ds(at, pair), :]
        for layer, h, count in chunks:
            tall = count * rows
            top = layer * per_layer + h * rows
            here = slice(top, top + tall)
            query = messages[layer][h * rows : h * rows + tall, :]
            grad = messages[layer][per_layer + h * rows : per_layer + h * rows + tall, :]
            total = jnp.concatenate([totals[here, :]] * (pair // 128), axis=1)
            dot = jnp.concatenate([dots[here, :]] * (pair // 128), axis=1)
            scores = lax.dot_general(query, key_tile, NT_DIMS, preferred_element_type=jnp.float32)
            weights = jnp.exp2(scores * (inv_root * LOG2E) - total)
            if masked:
                key_pos = lax.broadcasted_iota(jnp.int32, (1, pair), 1)
                query_pos = lax.broadcasted_iota(jnp.int32, (tall, 1), 0) % rows + x * rows
                weights = jnp.where(key_pos <= query_pos, weights, 0.0)
            weight_grads = lax.dot_general(
                grad, value_tile, NT_DIMS, preferred_element_type=jnp.float32
            )
            score_grads = weights * (weight_grads - dot) * inv_root
            weights_all[here, columns] = weights.astype(jnp.bfloat16)
            score_grads = score_grads.astype(jnp.bfloat16)
            score_all[here, columns] = score_grads
            if turned is not None:
                turned[columns, here] = jnp.transpose(score_grads)

    def leave(j, key_sum, value_sum):
        both = [jnp.transpose(total.astype(jnp.bfloat16)) for total in (key_sum, value_sum)]
        step = z - j
        for half in range(2):
            chosen = jnp.concatenate(
                [jnp.where(x == half, total[:rows], total[rows:]) for total in both], axis=1
            )

            @pl.when(step < near)
            def _():
                halves[2 * half][step] = chosen

            @pl.when(step >= near)
            def _():
                halves[2 * half + 1][step - near] = chosen

    def sweep(j, masked, query_acc):
        at = pl.multiple_of(j * pair, pair)
        here = slice(0, pair)
        tiles(at, here, masked)
        query_acc[...] += jnp.dot(
            score_all[:, here], keys[pl.ds(at, pair), :], preferred_element_type=jnp.float32
        )
        leave(
            j,
            jnp.dot(query_turned[...], score_all[:, here], preferred_element_type=jnp.float32),
            jnp.dot(grad_turned[...], weights_all[:, here], preferred_element_type=jnp.float32),
        )

    def stepwise():
        query_acc = refs[0]
        query_acc[...] = jnp.zeros_like(query_acc)

        def full(j, carry):
            sweep(j, False, query_acc)
            return carry

        lax.fori_loop(0, z, full, 0)
        sweep(z, True, query_acc)
        for layer in range(layers):
            query_outs[layer][...] = query_acc[
                layer * per_layer : (layer + 1) * per_layer, :
            ].astype(jnp.bfloat16)

    def whole():
        score_turned = refs[1]
        for j in range(outer):
            here = slice(j * pair, (j + 1) * pair)
            tiles(j * pair, here, j == outer - 1, score_turned)
        key_sum = jnp.dot(query_turned[...], score_all[...], preferred_element_type=jnp.float32)
        value_sum = jnp.dot(grad_turned[...], weights_all[...], preferred_element_type=jnp.float32)
        for j in range(outer):
            here = slice(j * pair, (j + 1) * pair)
            leave(j, key_sum[:, here], value_sum[:, here])
        key_turned = jnp.transpose(keys[...])
        for layer in range(layers):
            there = slice(layer * per_layer, (layer + 1) * per_layer)
            total = jnp.dot(
                key_turned, score_turned[:, there], preferred_element_type=jnp.float32
            )
            query_outs[layer][...] = jnp.transpose(total.astype(jnp.bfloat16))

    if outer <= UNROLLED:
        pl.when(z == outer - 1)(whole)
        pl.when(z < outer - 1)(stepwise)
    else:
        stepwise()

    def blank(out, first):
        def body(k, carry):
            out[k - first] = jnp.zeros(out.shape[1:], jnp.bfloat16)
            return carry

        lax.fori_loop(jnp.maximum(z + 1, first), first + out.shape[0], body, 0)

    for half in range(2):
        blank(halves[2 * half], 0)
        blank(halves[2 * half + 1], near)


def add_kernel(mine, theirs, *outs):
    for k, out in enumerate(outs):
        out[...] = (mine[k].astype(jnp.float32) + theirs[k].astype(jnp.float32)).astype(
            jnp.bfloat16
        )


def place_kernel(heads, head, place_ref, *refs):
    messages, out = refs[:-1], refs[-1]
    rows = out.shape[0]
    for k, message in enumerate(messages):
        start = pl.multiple_of((place_ref[0] ^ k) * heads * head, 128)
        for h in range(heads):
            at = pl.multiple_of(start + h * head, 128)
            out[:, pl.ds(at, head)] = message[h * rows : (h + 1) * rows, :]


def total_kernel(*refs):
    blocks, key_out, value_out = refs[:-2], refs[-2], refs[-1]
    total = blocks[0][...].astype(jnp.float32)
    for block in blocks[1:]:
        total = total + block[...].astype(jnp.float32)
    head = key_out.shape[1]
    key_out[...] = total[:, :head].astype(jnp.bfloat16)
    value_out[...] = total[:, head:].astype(jnp.bfloat16)


def call(kernel, outs, in_specs, scratch=(), limit=VMEM_LIMIT, out_specs=None):
    return pl.pallas_call(
        kernel,
        out_shape=[jax.ShapeDtypeStruct(shape, jnp.bfloat16) for shape in outs],
        in_specs=in_specs,
        out_specs=out_specs or [VMEM] * len(outs),
        scratch_shapes=list(scratch),
        compiler_params=pltpu.CompilerParams(vmem_limit_bytes=limit),
    )


def swap(array, axis, bits):
    size = lax.axis_size(axis)
    return lax.ppermute(array, axis, [(i, i ^ bits) for i in range(size)])


def move(array, step):
    size = lax.axis_size("seq")
    return lax.ppermute(
        array, "seq", [(i, i + step) for i in range(size) if 0 <= i + step < size]
    )


def local(queries, cache_keys, cache_values, saved_out, out_grads, log_sums):
    sections = lax.axis_size("section")
    seq = lax.axis_size("seq")
    outer = seq // 2
    section_at = lax.axis_index("section").astype(jnp.int32).reshape(1)
    seq_at = lax.axis_index("seq").astype(jnp.int32)
    rows, head = cache_keys.shape
    heads = log_sums.shape[2] // sections
    inv_root = 1.0 / math.sqrt(head)
    info = jnp.stack([seq_at // 2, seq_at % 2])
    lines = 2 * heads * rows + up16(EXTRA * heads)

    totals = jnp.transpose(log_sums[0])

    half = sections // 2
    *sent, own = call(
        functools.partial(pack_kernel, heads, head, tuple(range(sections)), 2, 0),
        [(lines, 128)] * sections + [(rows, 2 * head)],
        [SMEM] + [HBM] * 6,
        [
            pltpu.VMEM((sections, 3, rows, heads * head), jnp.bfloat16),
            pltpu.VMEM(totals.shape, jnp.bfloat16),
            pltpu.VMEM((sections, lines, 128), jnp.bfloat16),
            pltpu.SemaphoreType.DMA((4 * sections + 3,)),
        ],
        limit=PACK_LIMIT,
        out_specs=[HBM] * (sections + 1),
    )(section_at, queries[0], out_grads[0], saved_out[0], totals, cache_keys, cache_values)
    passed = swap(sent[half + 1], "section", 1)
    messages = [sent[0], swap(sent[1], "section", 1), swap(sent[half], "section", half)]
    passed, tied = lax.optimization_barrier((passed, own))
    messages.append(swap(passed, "section", half))

    def exchange(own):
        far = {k: swap(own, "seq", 2 * k) for k in reversed(range(1, outer))}
        return jnp.stack([far[k] for k in range(1, outer)])

    def nothing(own):
        return jnp.zeros((outer - 1, *own.shape), own.dtype)

    further = lax.cond(seq_at >= 0, exchange, nothing, tied)
    blocks_here = [own, swap(own, "seq", 1), further, swap(further, "seq", 1)]

    every = sections * heads * rows
    across = 2 * rows * (outer if outer <= UNROLLED else 1)
    bf16 = functools.partial(pltpu.VMEM, dtype=jnp.bfloat16)
    mine_near, mine_far, theirs_near, theirs_far, *back = call(
        functools.partial(attend_kernel, sections, heads, head, outer, inv_root),
        [(outer // 2, rows, 2 * head), (outer - outer // 2, rows, 2 * head)] * 2
        + [(heads * rows, head)] * sections,
        [SMEM] + [VMEM] * (sections + 4),
        [bf16((seq * rows, head))] * 2
        + [bf16((head, every))] * 2
        + [pltpu.VMEM((every, 128), jnp.float32)] * 2
        + [bf16((every, across))] * 2
        + [pltpu.VMEM((every, head), jnp.float32)]
        + ([bf16((across, every))] if outer <= UNROLLED else []),
    )(info, *messages, *blocks_here)

    def reduced(mine, theirs):
        count = mine.shape[0]
        return call(add_kernel, [(rows, 2 * head)] * count, [VMEM] * 2)(
            mine, swap(theirs, "seq", 1)
        )

    far_sums = reduced(mine_far, theirs_far)
    summed = [*reduced(mine_near, theirs_near), *far_sums]
    blocks = [move(summed[k], -2 * k) for k in reversed(range(1, outer))] + [summed[0]]
    back[1:] = lax.optimization_barrier((swap(back[1], "section", 1), *back[2:]))
    back[2:] = [swap(back[k], "section", k) for k in range(2, sections)]
    (query_grads,) = call(
        functools.partial(place_kernel, heads, head),
        [queries.shape[1:]],
        [SMEM] + [VMEM] * sections,
    )(section_at, *back)
    blocks[0], query_grads = lax.optimization_barrier((blocks[0], query_grads))
    key_grads, value_grads = call(total_kernel, [(rows, head)] * 2, [VMEM] * outer)(*blocks)
    return (query_grads[None], key_grads, value_grads)


def solution(mesh):
    placed = (
        P("section", "seq", None),
        P("seq", "section"),
        P("seq", "section"),
        P("section", "seq", None),
        P("section", "seq", None),
        P("section", "seq", None),
    )
    return jax.shard_map(
        local,
        mesh=mesh,
        in_specs=placed,
        out_specs=(P("section", "seq", None), P("seq", "section"), P("seq", "section")),
        check_vma=False,
    )
```

```python
import functools
import math

import jax
import jax.numpy as jnp
from jax import lax
from jax.experimental import pallas as pl
from jax.experimental.pallas import tpu as pltpu
from jax.sharding import PartitionSpec as P

NT_DIMS = (((1,), (1,)), ((), ()))
UNROLLED = 4
EXTRA = 4
VMEM_LIMIT = 32 * 1024 * 1024
PACK_LIMIT = 62 * 1024 * 1024
LOG2E = math.log2(math.e)
VMEM = pl.BlockSpec(memory_space=pltpu.VMEM)
HBM = pl.BlockSpec(memory_space=pltpu.HBM)


def up16(rows):
    return -(-rows // 16) * 16


def pack_kernel(heads, head, which, cached, after, queries, grads, saved, totals, *refs):
    cache, refs = refs[:cached], refs[cached + after :]
    outs, refs = refs[: len(which)], refs[len(which) :]
    block, refs = (refs[0], refs[1:]) if cached else (None, refs)
    here, totals_here, ready, sems = refs
    rows = queries.shape[0]
    here_at = lax.axis_index("section")
    width = heads * head
    groups = queries.shape[1] // width
    ends = []
    for m, k in enumerate(which):
        columns = pl.ds(pl.multiple_of((here_at ^ k) * width, 128), width)
        for i, source in enumerate((grads, saved, queries)):
            ends.append((source.at[:, columns], here.at[m, i]))
    ends.append((totals, totals_here))
    for i, source in enumerate(cache):
        ends.append((source, block.at[:, pl.ds(i * head, head)]))
    loads = [pltpu.make_async_copy(*pair, sems.at[i]) for i, pair in enumerate(ends)]
    stores = [
        pltpu.make_async_copy(ready.at[m], out, sems.at[len(loads) + m])
        for m, out in enumerate(outs)
    ]
    for load in loads:
        load.start()
    lanes = lax.broadcasted_iota(jnp.int32, (rows, 128), 1)
    for m, k in enumerate(which):
        message = ready.at[m]
        for load in loads[3 * m : 3 * m + 3]:
            load.wait()
        dots = jnp.zeros((rows, 128), jnp.float32)
        for h in range(heads):
            columns = slice(h * head, (h + 1) * head)
            grad = here[m, 0, :, columns]
            out = here[m, 1, :, columns].astype(jnp.float32)
            product = grad.astype(jnp.float32) * out
            dots = jnp.where(lanes == h, jnp.sum(product, axis=1, keepdims=True), dots)
            message[h * rows : (h + 1) * rows, :] = here[m, 2, :, columns]
            message[(heads + h) * rows : (heads + h + 1) * rows, :] = grad
        dots = jnp.transpose(dots)[:heads]
        high = dots.astype(jnp.bfloat16).astype(jnp.float32)
        rest = dots - high
        middle = rest.astype(jnp.bfloat16).astype(jnp.float32)
        low = rest - middle
        if m == 0:
            loads[3 * len(which)].wait()
        chosen = totals_here[0:heads, :].astype(jnp.float32)
        for group in range(1, groups):
            part = totals_here[group * heads : (group + 1) * heads, :].astype(jnp.float32)
            chosen = jnp.where((here_at ^ k) == group, part, chosen)
        spare = jnp.zeros((message.shape[0] - 2 * heads * rows - EXTRA * heads, 128), jnp.float32)
        extra = jnp.concatenate([chosen, high, middle, low, spare], axis=0)
        message[2 * heads * rows :, :] = extra.astype(jnp.bfloat16)
        stores[m].start()
    for copy in loads[3 * len(which) + 1 :] + stores:
        copy.wait()


def attend_kernel(layers, heads, head, outer, inv_root, *refs):
    messages = refs[:layers]
    own, own_swapped, further, others = refs[layers : layers + 4]
    refs = refs[layers + 4 :]
    halves, refs = refs[:4], refs[4:]
    query_outs, refs = refs[:layers], refs[layers:]
    keys, values, query_turned, grad_turned, totals, dots, weights_all, score_all, *refs = refs
    rows = own.shape[0]
    pair = 2 * rows
    at_seq = lax.axis_index("seq")
    z, x = at_seq // 2, at_seq % 2
    near = outer // 2
    per_layer = heads * rows
    every = layers * per_layer
    for k in range(outer):
        at = pl.multiple_of((z ^ k) * pair, pair)
        here, there = (further.at[k - 1], others.at[k - 1]) if k else (own, own_swapped)
        for block, half in ((here, x), (there, 1 - x)):
            keys[pl.ds(at + half * rows, rows), :] = block[:, :head]
            values[pl.ds(at + half * rows, rows), :] = block[:, head:]

    for layer in range(layers):
        there = slice(layer * per_layer, (layer + 1) * per_layer)
        query_turned[:, there] = jnp.transpose(messages[layer][:per_layer, :])
        grad_turned[:, there] = jnp.transpose(messages[layer][per_layer : 2 * per_layer, :])
        extra = messages[layer][2 * per_layer :, :].astype(jnp.float32)
        high, middle, low = (extra[i * heads : (i + 1) * heads] for i in (1, 2, 3))
        spare = jnp.zeros((128 - 2 * heads, 128), jnp.float32)
        columns = jnp.transpose(
            jnp.concatenate([extra[:heads] * LOG2E, high + (middle + low), spare], axis=0)
        )
        for h in range(heads):
            at = layer * per_layer + h * rows
            totals[at : at + rows, :] = jnp.broadcast_to(columns[:, h : h + 1], (rows, 128))
            dots[at : at + rows, :] = jnp.broadcast_to(
                columns[:, heads + h : heads + h + 1], (rows, 128)
            )
    chunks = [
        (layer, h, min(2, heads - h)) for layer in range(layers) for h in range(0, heads, 2)
    ]

    def tiles(at, columns, masked, turned=None):
        key_tile = keys[pl.ds(at, pair), :]
        value_tile = values[pl.ds(at, pair), :]
        for layer, h, count in chunks:
            tall = count * rows
            top = layer * per_layer + h * rows
            here = slice(top, top + tall)
            query = messages[layer][h * rows : h * rows + tall, :]
            grad = messages[layer][per_layer + h * rows : per_layer + h * rows + tall, :]
            total = jnp.concatenate([totals[here, :]] * (pair // 128), axis=1)
            dot = jnp.concatenate([dots[here, :]] * (pair // 128), axis=1)
            scores = lax.dot_general(query, key_tile, NT_DIMS, preferred_element_type=jnp.float32)
            weights = jnp.exp2(scores * (inv_root * LOG2E) - total)
            if masked:
                key_pos = lax.broadcasted_iota(jnp.int32, (1, pair), 1)
                query_pos = lax.broadcasted_iota(jnp.int32, (tall, 1), 0) % rows + x * rows
                weights = jnp.where(key_pos <= query_pos, weights, 0.0)
            weight_grads = lax.dot_general(
                grad, value_tile, NT_DIMS, preferred_element_type=jnp.float32
            )
            score_grads = weights * (weight_grads - dot) * inv_root
            weights_all[here, columns] = weights.astype(jnp.bfloat16)
            score_grads = score_grads.astype(jnp.bfloat16)
            score_all[here, columns] = score_grads
            if turned is not None:
                turned[columns, here] = jnp.transpose(score_grads)

    def leave(step, key_sum, value_sum):
        both = [jnp.transpose(total.astype(jnp.bfloat16)) for total in (key_sum, value_sum)]
        for half in range(2):
            chosen = jnp.concatenate(
                [jnp.where(x == half, total[:rows], total[rows:]) for total in both], axis=1
            )
            if isinstance(step, int):
                halves[2 * half + (step >= near)][step - near * (step >= near)] = chosen
                continue

            @pl.when(step < near)
            def _():
                halves[2 * half][step] = chosen

            @pl.when(step >= near)
            def _():
                halves[2 * half + 1][step - near] = chosen

    def sweep(j, masked, query_acc):
        at = pl.multiple_of(j * pair, pair)
        here = slice(0, pair)
        tiles(at, here, masked)
        query_acc[...] += jnp.dot(
            score_all[:, here], keys[pl.ds(at, pair), :], preferred_element_type=jnp.float32
        )
        leave(
            z - j,
            jnp.dot(query_turned[...], score_all[:, here], preferred_element_type=jnp.float32),
            jnp.dot(grad_turned[...], weights_all[:, here], preferred_element_type=jnp.float32),
        )

    def stepwise():
        query_acc = refs[0]
        query_acc[...] = jnp.zeros_like(query_acc)

        def full(j, carry):
            sweep(j, False, query_acc)
            return carry

        lax.fori_loop(0, z, full, 0)
        sweep(z, True, query_acc)
        for layer in range(layers):
            query_outs[layer][...] = query_acc[
                layer * per_layer : (layer + 1) * per_layer, :
            ].astype(jnp.bfloat16)

    def whole():
        score_turned = refs[1]
        for j in range(outer):
            here = slice(j * pair, (j + 1) * pair)
            tiles(j * pair, here, j == outer - 1, score_turned)
        key_sum = jnp.dot(query_turned[...], score_all[...], preferred_element_type=jnp.float32)
        value_sum = jnp.dot(grad_turned[...], weights_all[...], preferred_element_type=jnp.float32)
        for j in range(outer):
            here = slice(j * pair, (j + 1) * pair)
            leave(outer - 1 - j, key_sum[:, here], value_sum[:, here])
        key_turned = jnp.transpose(keys[...])
        for layer in range(layers):
            there = slice(layer * per_layer, (layer + 1) * per_layer)
            total = jnp.dot(
                key_turned, score_turned[:, there], preferred_element_type=jnp.float32
            )
            query_outs[layer][...] = jnp.transpose(total.astype(jnp.bfloat16))

    if outer <= UNROLLED:
        pl.when(z == outer - 1)(whole)
        pl.when(z < outer - 1)(stepwise)
    else:
        stepwise()

    def blank(out, first):
        def body(k, carry):
            out[k - first] = jnp.zeros(out.shape[1:], jnp.bfloat16)
            return carry

        lax.fori_loop(jnp.maximum(z + 1, first), first + out.shape[0], body, 0)

    for half in range(2):
        blank(halves[2 * half], 0)
        blank(halves[2 * half + 1], near)


def add_kernel(mine, theirs, *outs):
    for k, out in enumerate(outs):
        out[...] = (mine[k].astype(jnp.float32) + theirs[k].astype(jnp.float32)).astype(
            jnp.bfloat16
        )


def place_kernel(heads, head, *refs):
    messages, out = refs[:-1], refs[-1]
    rows = out.shape[0]
    here_at = lax.axis_index("section")
    for k, message in enumerate(messages):
        start = pl.multiple_of((here_at ^ k) * heads * head, 128)
        for h in range(heads):
            at = pl.multiple_of(start + h * head, 128)
            out[:, pl.ds(at, head)] = message[h * rows : (h + 1) * rows, :]


def total_kernel(*refs):
    blocks, key_out, value_out = refs[:-2], refs[-2], refs[-1]
    total = blocks[0][...].astype(jnp.float32)
    for block in blocks[1:]:
        total = total + block[...].astype(jnp.float32)
    head = key_out.shape[1]
    key_out[...] = total[:, :head].astype(jnp.bfloat16)
    value_out[...] = total[:, head:].astype(jnp.bfloat16)


def call(kernel, outs, in_specs, scratch=(), limit=VMEM_LIMIT, out_specs=None):
    return pl.pallas_call(
        kernel,
        out_shape=[jax.ShapeDtypeStruct(shape, jnp.bfloat16) for shape in outs],
        in_specs=in_specs,
        out_specs=out_specs or [VMEM] * len(outs),
        scratch_shapes=list(scratch),
        compiler_params=pltpu.CompilerParams(vmem_limit_bytes=limit),
    )


def swap(array, axis, bits):
    size = lax.axis_size(axis)
    return lax.ppermute(array, axis, [(i, i ^ bits) for i in range(size)])


def move(array, step):
    size = lax.axis_size("seq")
    return lax.ppermute(
        array, "seq", [(i, i + step) for i in range(size) if 0 <= i + step < size]
    )


def local(queries, cache_keys, cache_values, saved_out, out_grads, log_sums):
    sections = lax.axis_size("section")
    seq = lax.axis_size("seq")
    outer = seq // 2
    seq_at = lax.axis_index("seq").astype(jnp.int32)
    rows, head = cache_keys.shape
    heads = log_sums.shape[2] // sections
    inv_root = 1.0 / math.sqrt(head)
    lines = 2 * heads * rows + up16(EXTRA * heads)

    totals = jnp.transpose(log_sums[0])

    half = sections // 2
    *sent, own = call(
        functools.partial(pack_kernel, heads, head, tuple(range(sections)), 2, 0),
        [(lines, 128)] * sections + [(rows, 2 * head)],
        [HBM] * 6,
        [
            pltpu.VMEM((sections, 3, rows, heads * head), jnp.bfloat16),
            pltpu.VMEM(totals.shape, jnp.bfloat16),
            pltpu.VMEM((sections, lines, 128), jnp.bfloat16),
            pltpu.SemaphoreType.DMA((4 * sections + 3,)),
        ],
        limit=PACK_LIMIT,
        out_specs=[HBM] * (sections + 1),
    )(queries[0], out_grads[0], saved_out[0], totals, cache_keys, cache_values)
    passed = swap(sent[half + 1], "section", 1)
    messages = [sent[0], swap(sent[1], "section", 1), swap(sent[half], "section", half)]
    passed, tied = lax.optimization_barrier((passed, own))
    messages.append(swap(passed, "section", half))

    def exchange(own):
        far = {k: swap(own, "seq", 2 * k) for k in reversed(range(1, outer))}
        return jnp.stack([far[k] for k in range(1, outer)])

    def nothing(own):
        return jnp.zeros((outer - 1, *own.shape), own.dtype)

    further = lax.cond(seq_at >= 0, exchange, nothing, tied)
    blocks_here = [own, swap(own, "seq", 1), further, swap(further, "seq", 1)]

    every = sections * heads * rows
    across = 2 * rows * (outer if outer <= UNROLLED else 1)
    bf16 = functools.partial(pltpu.VMEM, dtype=jnp.bfloat16)
    mine_near, mine_far, theirs_near, theirs_far, *back = call(
        functools.partial(attend_kernel, sections, heads, head, outer, inv_root),
        [(outer // 2, rows, 2 * head), (outer - outer // 2, rows, 2 * head)] * 2
        + [(heads * rows, head)] * sections,
        [VMEM] * (sections + 4),
        [bf16((seq * rows, head))] * 2
        + [bf16((head, every))] * 2
        + [pltpu.VMEM((every, 128), jnp.float32)] * 2
        + [bf16((every, across))] * 2
        + [pltpu.VMEM((every, head), jnp.float32)]
        + ([bf16((across, every))] if outer <= UNROLLED else []),
    )(*messages, *blocks_here)

    def reduced(mine, theirs):
        count = mine.shape[0]
        return call(add_kernel, [(rows, 2 * head)] * count, [VMEM] * 2)(
            mine, swap(theirs, "seq", 1)
        )

    far_sums = reduced(mine_far, theirs_far)
    summed = [*reduced(mine_near, theirs_near), *far_sums]
    blocks = [move(summed[k], -2 * k) for k in reversed(range(1, outer))] + [summed[0]]
    back[1:] = lax.optimization_barrier((swap(back[1], "section", 1), *back[2:]))
    back[2:] = [swap(back[k], "section", k) for k in range(2, sections)]
    (query_grads,) = call(
        functools.partial(place_kernel, heads, head),
        [queries.shape[1:]],
        [VMEM] * sections,
    )(*back)
    blocks[0], query_grads = lax.optimization_barrier((blocks[0], query_grads))
    key_grads, value_grads = call(total_kernel, [(rows, head)] * 2, [VMEM] * outer)(*blocks)
    return (query_grads[None], key_grads, value_grads)


def solution(mesh):
    placed = (
        P("section", "seq", None),
        P("seq", "section"),
        P("seq", "section"),
        P("section", "seq", None),
        P("section", "seq", None),
        P("section", "seq", None),
    )
    return jax.shard_map(
        local,
        mesh=mesh,
        in_specs=placed,
        out_specs=(P("section", "seq", None), P("seq", "section"), P("seq", "section")),
        check_vma=False,
    )
```

```python
import functools
import math

import jax
import jax.numpy as jnp
from jax import lax
from jax.experimental import pallas as pl
from jax.experimental.pallas import tpu as pltpu
from jax.sharding import PartitionSpec as P

NT_DIMS = (((1,), (1,)), ((), ()))
UNROLLED = 4
EXTRA = 4
VMEM_LIMIT = 32 * 1024 * 1024
PACK_LIMIT = 62 * 1024 * 1024
LOG2E = math.log2(math.e)
VMEM = pl.BlockSpec(memory_space=pltpu.VMEM)
HBM = pl.BlockSpec(memory_space=pltpu.HBM)


def up16(rows):
    return -(-rows // 16) * 16


def pack_kernel(heads, head, which, cached, after, queries, grads, saved, totals, *refs):
    cache, refs = refs[:cached], refs[cached + after :]
    outs, refs = refs[: len(which)], refs[len(which) :]
    block, refs = (refs[0], refs[1:]) if cached else (None, refs)
    here, ready, sems = refs
    rows = queries.shape[0]
    here_at = lax.axis_index("section")
    width = heads * head
    groups = queries.shape[1] // width
    ends = []
    for m, k in enumerate(which):
        columns = pl.ds(pl.multiple_of((here_at ^ k) * width, 128), width)
        for i, source in enumerate((grads, saved, queries)):
            ends.append((source.at[:, columns], here.at[m, i]))
    for i, source in enumerate(cache):
        ends.append((source, block.at[:, pl.ds(i * head, head)]))
    loads = [pltpu.make_async_copy(*pair, sems.at[i]) for i, pair in enumerate(ends)]
    stores = [
        pltpu.make_async_copy(ready.at[m], out, sems.at[len(loads) + m])
        for m, out in enumerate(outs)
    ]
    for load in loads:
        load.start()
    lanes = lax.broadcasted_iota(jnp.int32, (rows, 128), 1)
    for m, k in enumerate(which):
        message = ready.at[m]
        for load in loads[3 * m : 3 * m + 3]:
            load.wait()
        dots = jnp.zeros((rows, 128), jnp.float32)
        for h in range(heads):
            columns = slice(h * head, (h + 1) * head)
            grad = here[m, 0, :, columns]
            out = here[m, 1, :, columns].astype(jnp.float32)
            product = grad.astype(jnp.float32) * out
            dots = jnp.where(lanes == h, jnp.sum(product, axis=1, keepdims=True), dots)
            message[h * rows : (h + 1) * rows, :] = here[m, 2, :, columns]
            message[(heads + h) * rows : (heads + h + 1) * rows, :] = grad
        dots = jnp.transpose(dots)[:heads]
        high = dots.astype(jnp.bfloat16).astype(jnp.float32)
        rest = dots - high
        middle = rest.astype(jnp.bfloat16).astype(jnp.float32)
        low = rest - middle
        every_total = totals[...].astype(jnp.float32)
        chosen = every_total[0:heads]
        for group in range(1, groups):
            part = every_total[group * heads : (group + 1) * heads]
            chosen = jnp.where((here_at ^ k) == group, part, chosen)
        spare = jnp.zeros((message.shape[0] - 2 * heads * rows - EXTRA * heads, 128), jnp.float32)
        extra = jnp.concatenate([chosen, high, middle, low, spare], axis=0)
        message[2 * heads * rows :, :] = extra.astype(jnp.bfloat16)
        stores[m].start()
    for copy in loads[3 * len(which) :] + stores:
        copy.wait()


def attend_kernel(layers, heads, head, outer, inv_root, *refs):
    messages = refs[:layers]
    own, own_swapped, further, others = refs[layers : layers + 4]
    refs = refs[layers + 4 :]
    halves, refs = refs[:4], refs[4:]
    query_outs, refs = refs[:layers], refs[layers:]
    keys, values, query_turned, grad_turned, totals, dots, weights_all, score_all, *refs = refs
    rows = own.shape[0]
    pair = 2 * rows
    at_seq = lax.axis_index("seq")
    z, x = at_seq // 2, at_seq % 2
    near = outer // 2
    per_layer = heads * rows
    every = layers * per_layer
    for k in range(outer):
        at = pl.multiple_of((z ^ k) * pair, pair)
        here, there = (further.at[k - 1], others.at[k - 1]) if k else (own, own_swapped)
        for block, half in ((here, x), (there, 1 - x)):
            keys[pl.ds(at + half * rows, rows), :] = block[:, :head]
            values[pl.ds(at + half * rows, rows), :] = block[:, head:]

    for layer in range(layers):
        there = slice(layer * per_layer, (layer + 1) * per_layer)
        query_turned[:, there] = jnp.transpose(messages[layer][:per_layer, :])
        grad_turned[:, there] = jnp.transpose(messages[layer][per_layer : 2 * per_layer, :])
        extra = messages[layer][2 * per_layer :, :].astype(jnp.float32)
        high, middle, low = (extra[i * heads : (i + 1) * heads] for i in (1, 2, 3))
        spare = jnp.zeros((128 - 2 * heads, 128), jnp.float32)
        columns = jnp.transpose(
            jnp.concatenate([extra[:heads] * LOG2E, high + (middle + low), spare], axis=0)
        )
        for h in range(heads):
            at = layer * per_layer + h * rows
            totals[at : at + rows, :] = jnp.broadcast_to(columns[:, h : h + 1], (rows, 128))
            dots[at : at + rows, :] = jnp.broadcast_to(
                columns[:, heads + h : heads + h + 1], (rows, 128)
            )
    chunks = [
        (layer, h, min(2, heads - h)) for layer in range(layers) for h in range(0, heads, 2)
    ]

    def tiles(at, columns, masked, turned=None):
        key_tile = keys[pl.ds(at, pair), :]
        value_tile = values[pl.ds(at, pair), :]
        for layer, h, count in chunks:
            tall = count * rows
            top = layer * per_layer + h * rows
            here = slice(top, top + tall)
            query = messages[layer][h * rows : h * rows + tall, :]
            grad = messages[layer][per_layer + h * rows : per_layer + h * rows + tall, :]
            total = jnp.concatenate([totals[here, :]] * (pair // 128), axis=1)
            dot = jnp.concatenate([dots[here, :]] * (pair // 128), axis=1)
            scores = lax.dot_general(query, key_tile, NT_DIMS, preferred_element_type=jnp.float32)
            weights = jnp.exp2(scores * (inv_root * LOG2E) - total)
            if masked:
                key_pos = lax.broadcasted_iota(jnp.int32, (1, pair), 1)
                query_pos = lax.broadcasted_iota(jnp.int32, (tall, 1), 0) % rows + x * rows
                weights = jnp.where(key_pos <= query_pos, weights, 0.0)
            weight_grads = lax.dot_general(
                grad, value_tile, NT_DIMS, preferred_element_type=jnp.float32
            )
            score_grads = weights * (weight_grads - dot) * inv_root
            weights_all[here, columns] = weights.astype(jnp.bfloat16)
            score_grads = score_grads.astype(jnp.bfloat16)
            score_all[here, columns] = score_grads
            if turned is not None:
                turned[columns, here] = jnp.transpose(score_grads)

    def leave(step, key_sum, value_sum):
        both = [jnp.transpose(total.astype(jnp.bfloat16)) for total in (key_sum, value_sum)]
        for half in range(2):
            chosen = jnp.concatenate(
                [jnp.where(x == half, total[:rows], total[rows:]) for total in both], axis=1
            )
            if isinstance(step, int):
                halves[2 * half + (step >= near)][step - near * (step >= near)] = chosen
                continue

            @pl.when(step < near)
            def _():
                halves[2 * half][step] = chosen

            @pl.when(step >= near)
            def _():
                halves[2 * half + 1][step - near] = chosen

    def sweep(j, masked, query_acc):
        at = pl.multiple_of(j * pair, pair)
        here = slice(0, pair)
        tiles(at, here, masked)
        query_acc[...] += jnp.dot(
            score_all[:, here], keys[pl.ds(at, pair), :], preferred_element_type=jnp.float32
        )
        leave(
            z - j,
            jnp.dot(query_turned[...], score_all[:, here], preferred_element_type=jnp.float32),
            jnp.dot(grad_turned[...], weights_all[:, here], preferred_element_type=jnp.float32),
        )

    def stepwise():
        query_acc = refs[0]
        query_acc[...] = jnp.zeros_like(query_acc)

        def full(j, carry):
            sweep(j, False, query_acc)
            return carry

        lax.fori_loop(0, z, full, 0)
        sweep(z, True, query_acc)
        for layer in range(layers):
            query_outs[layer][...] = query_acc[
                layer * per_layer : (layer + 1) * per_layer, :
            ].astype(jnp.bfloat16)

    def whole():
        score_turned = refs[1]
        for j in range(outer):
            here = slice(j * pair, (j + 1) * pair)
            tiles(j * pair, here, j == outer - 1, score_turned)
        key_sum = jnp.dot(query_turned[...], score_all[...], preferred_element_type=jnp.float32)
        value_sum = jnp.dot(grad_turned[...], weights_all[...], preferred_element_type=jnp.float32)
        for j in range(outer):
            here = slice(j * pair, (j + 1) * pair)
            leave(outer - 1 - j, key_sum[:, here], value_sum[:, here])
        key_turned = jnp.transpose(keys[...])
        for layer in range(layers):
            there = slice(layer * per_layer, (layer + 1) * per_layer)
            total = jnp.dot(
                key_turned, score_turned[:, there], preferred_element_type=jnp.float32
            )
            query_outs[layer][...] = jnp.transpose(total.astype(jnp.bfloat16))

    if outer <= UNROLLED:
        pl.when(z == outer - 1)(whole)
        pl.when(z < outer - 1)(stepwise)
    else:
        stepwise()

    def blank(out, first):
        def body(k, carry):
            out[k - first] = jnp.zeros(out.shape[1:], jnp.bfloat16)
            return carry

        lax.fori_loop(jnp.maximum(z + 1, first), first + out.shape[0], body, 0)

    for half in range(2):
        blank(halves[2 * half], 0)
        blank(halves[2 * half + 1], near)


def add_kernel(mine, theirs, *outs):
    for k, out in enumerate(outs):
        out[...] = (mine[k].astype(jnp.float32) + theirs[k].astype(jnp.float32)).astype(
            jnp.bfloat16
        )


def place_kernel(heads, head, *refs):
    messages, out = refs[:-1], refs[-1]
    rows = out.shape[0]
    here_at = lax.axis_index("section")
    for k, message in enumerate(messages):
        start = pl.multiple_of((here_at ^ k) * heads * head, 128)
        for h in range(heads):
            at = pl.multiple_of(start + h * head, 128)
            out[:, pl.ds(at, head)] = message[h * rows : (h + 1) * rows, :]


def total_kernel(*refs):
    blocks, key_out, value_out = refs[:-2], refs[-2], refs[-1]
    total = blocks[0][...].astype(jnp.float32)
    for block in blocks[1:]:
        total = total + block[...].astype(jnp.float32)
    head = key_out.shape[1]
    key_out[...] = total[:, :head].astype(jnp.bfloat16)
    value_out[...] = total[:, head:].astype(jnp.bfloat16)


def call(kernel, outs, in_specs, scratch=(), limit=VMEM_LIMIT, out_specs=None):
    return pl.pallas_call(
        kernel,
        out_shape=[jax.ShapeDtypeStruct(shape, jnp.bfloat16) for shape in outs],
        in_specs=in_specs,
        out_specs=out_specs or [VMEM] * len(outs),
        scratch_shapes=list(scratch),
        compiler_params=pltpu.CompilerParams(vmem_limit_bytes=limit),
    )


def swap(array, axis, bits):
    size = lax.axis_size(axis)
    return lax.ppermute(array, axis, [(i, i ^ bits) for i in range(size)])


def move(array, step):
    size = lax.axis_size("seq")
    return lax.ppermute(
        array, "seq", [(i, i + step) for i in range(size) if 0 <= i + step < size]
    )


def local(queries, cache_keys, cache_values, saved_out, out_grads, log_sums):
    sections = lax.axis_size("section")
    seq = lax.axis_size("seq")
    outer = seq // 2
    seq_at = lax.axis_index("seq").astype(jnp.int32)
    rows, head = cache_keys.shape
    heads = log_sums.shape[2] // sections
    inv_root = 1.0 / math.sqrt(head)
    lines = 2 * heads * rows + up16(EXTRA * heads)

    totals = jnp.transpose(log_sums[0])

    half = sections // 2
    *sent, own = call(
        functools.partial(pack_kernel, heads, head, tuple(range(sections)), 2, 0),
        [(lines, 128)] * sections + [(rows, 2 * head)],
        [HBM] * 3 + [VMEM] + [HBM] * 2,
        [
            pltpu.VMEM((sections, 3, rows, heads * head), jnp.bfloat16),
            pltpu.VMEM((sections, lines, 128), jnp.bfloat16),
            pltpu.SemaphoreType.DMA((4 * sections + 2,)),
        ],
        limit=PACK_LIMIT,
        out_specs=[HBM] * (sections + 1),
    )(queries[0], out_grads[0], saved_out[0], totals, cache_keys, cache_values)
    passed = swap(sent[half + 1], "section", 1)
    messages = [sent[0], swap(sent[1], "section", 1), swap(sent[half], "section", half)]
    passed, tied = lax.optimization_barrier((passed, own))
    messages.append(swap(passed, "section", half))

    def exchange(own):
        far = {k: swap(own, "seq", 2 * k) for k in reversed(range(1, outer))}
        return jnp.stack([far[k] for k in range(1, outer)])

    def nothing(own):
        return jnp.zeros((outer - 1, *own.shape), own.dtype)

    further = lax.cond(seq_at >= 0, exchange, nothing, tied)
    blocks_here = [own, swap(own, "seq", 1), further, swap(further, "seq", 1)]

    every = sections * heads * rows
    across = 2 * rows * (outer if outer <= UNROLLED else 1)
    bf16 = functools.partial(pltpu.VMEM, dtype=jnp.bfloat16)
    mine_near, mine_far, theirs_near, theirs_far, *back = call(
        functools.partial(attend_kernel, sections, heads, head, outer, inv_root),
        [(outer // 2, rows, 2 * head), (outer - outer // 2, rows, 2 * head)] * 2
        + [(heads * rows, head)] * sections,
        [VMEM] * (sections + 4),
        [bf16((seq * rows, head))] * 2
        + [bf16((head, every))] * 2
        + [pltpu.VMEM((every, 128), jnp.float32)] * 2
        + [bf16((every, across))] * 2
        + [pltpu.VMEM((every, head), jnp.float32)]
        + ([bf16((across, every))] if outer <= UNROLLED else []),
    )(*messages, *blocks_here)

    def reduced(mine, theirs):
        count = mine.shape[0]
        return call(add_kernel, [(rows, 2 * head)] * count, [VMEM] * 2)(
            mine, swap(theirs, "seq", 1)
        )

    far_sums = reduced(mine_far, theirs_far)
    summed = [*reduced(mine_near, theirs_near), *far_sums]
    blocks = [move(summed[k], -2 * k) for k in reversed(range(1, outer))] + [summed[0]]
    back[1:] = lax.optimization_barrier((swap(back[1], "section", 1), *back[2:]))
    back[2:] = [swap(back[k], "section", k) for k in range(2, sections)]
    (query_grads,) = call(
        functools.partial(place_kernel, heads, head),
        [queries.shape[1:]],
        [VMEM] * sections,
    )(*back)
    blocks[0], query_grads = lax.optimization_barrier((blocks[0], query_grads))
    key_grads, value_grads = call(total_kernel, [(rows, head)] * 2, [VMEM] * outer)(*blocks)
    return (query_grads[None], key_grads, value_grads)


def solution(mesh):
    placed = (
        P("section", "seq", None),
        P("seq", "section"),
        P("seq", "section"),
        P("section", "seq", None),
        P("section", "seq", None),
        P("section", "seq", None),
    )
    return jax.shard_map(
        local,
        mesh=mesh,
        in_specs=placed,
        out_specs=(P("section", "seq", None), P("seq", "section"), P("seq", "section")),
        check_vma=False,
    )
```
